32 devices in a mesh: row: 8 (over z, x), col: 4 (over y, core).
Axes of the slice: x: 2, y: 2, z: 4, core: 2. Of those that a mesh axis runs over, the one named last changes fastest.
Arguments:
- x_points: bfloat16 [8192, 64], P(('row', 'col')), may hold values from -6 to 6
- y_points: bfloat16 [32768, 64], P(('col', 'row')), may hold values from -6 to 6
- row_mass: bfloat16 [8192], P(('row', 'col')), may hold values from 1 to 30, as said below
- col_mass: bfloat16 [32768], P(('col', 'row')), may hold values from 1 to 30, as said below
- multipliers: bfloat16 [8192, 64], P(('row', 'col')), may hold values from -12 to 12
- col_potential: bfloat16 [32768], P(('col', 'row')), may hold values from -3 to 3
- basket: float32 [64], replicated, may hold values from 0.05 to 0.25
- damping: float32 [64], replicated, may hold values from 0.3 to 1.5
Outputs:
- row_potential: float32 [8192], P('row')
- col_potential_new: float32 [32768], P('col')
- multipliers_new: float32 [8192, 64], P(('row', 'col'))
The draws below stay inside these ranges and needn't reach their ends.
Inputs may be any that keep to these rules, and one draw needn't show every extreme that they name: `row_mass`: weights rise along the points' order by up to a factor of three. `col_mass`: weights rise along the points' order by up to a factor of three.
All inputs are finite; a program needn't handle non-finite values.
Results may differ from the reference program's by a relative error of at most 0.0012.
Values may be sent and summed in bfloat16 or wider, within the bound.
A program may use at most 64 MiB of HBM per device.

```python
import math
import jax
import jax.numpy as jnp
from jax import lax

A = 64
NX = 8192
NY = 32768


def rising_weights(key, count):
    base = jax.random.uniform(key, (count,), jnp.float32)
    scale = jnp.exp(base * jnp.log(10.0))
    ramp = 1.0 + 2.0 * jnp.arange(count, dtype=jnp.float32) / (count - 1)
    return scale * ramp


def draw_row_mass(key, part):
    return rising_weights(jax.random.fold_in(key, 11), NX).astype(jnp.bfloat16)


def draw_col_mass(key, part):
    return rising_weights(jax.random.fold_in(key, 23), NY).astype(jnp.bfloat16)


def draw_multipliers(key, part):
    first_key = jax.random.fold_in(jax.random.fold_in(key, 37), 0)
    base = jax.random.truncated_normal(first_key, -4.0, 4.0, (NX, A), jnp.float32)
    scale = 0.1
    return (base * scale).astype(jnp.bfloat16)


def levels(stream_key, extent, shards, least, largest):
    level = 1.0
    for dim, blocks in shards:
        draws = jax.random.uniform(jax.random.fold_in(jax.random.fold_in(stream_key, 6), dim), (blocks,), jnp.float32, least / len(shards), largest / len(shards))
        level = level * jnp.repeat(jnp.exp(draws), extent[dim] // blocks).reshape((-1,) + (1,) * (len(extent) - 1 - dim))
    return level


def normal_values(stream_key, dims, deviation, bound, shards=(), kind=jnp.bfloat16):
    values = jax.random.normal(stream_key, dims, jnp.float32) * deviation
    if len(shards) > 0:
        values = levels(stream_key, dims, shards, -0.22, 0.18) * values
    return jnp.clip(values, min=-bound, max=bound).astype(kind)


def setup_inputs(seed: int = 0) -> dict:
    key_of = jax.random.split(jax.random.key(seed), 9)
    x_points = normal_values(key_of[0], (NX, A), 1.0, 6.0, ((0, 32),))
    y_points = normal_values(key_of[1], (NY, A), 1.0, 6.0, ((0, 32),))
    row_mass = draw_row_mass(jax.random.fold_in(key_of[8], 71), 0)
    col_mass = draw_col_mass(jax.random.fold_in(key_of[8], 71), 0)
    multipliers = draw_multipliers(jax.random.fold_in(key_of[8], 71), 0)
    col_potential = normal_values(key_of[5], (NY,), 0.5, 3.0, ((0, 32),))
    basket = jnp.clip(jax.random.uniform(key_of[6], (A,), jnp.float32, 0.05, 0.25), 0.05, 0.25)
    damping = jnp.clip(jnp.exp(jax.random.uniform(key_of[7], (A,), jnp.float32, math.log(0.3), math.log(1.5))), 0.3, 1.5)
    return {"x_points": x_points, "y_points": y_points, "row_mass": row_mass, "col_mass": col_mass, "multipliers": multipliers, "col_potential": col_potential, "basket": basket, "damping": damping}


EPS = 0.5
KAPPA = 0.5
RIDGE = 1.0


def prepare_rows(x_rows, mult_rows, basket):
    xf = x_rows.astype(jnp.float32)
    hf = mult_rows.astype(jnp.float32)
    width = xf.shape[1]
    query = hf + (2.0 * KAPPA / width) * xf
    row_term = -jnp.sum(hf * xf, axis=1) - (KAPPA / width) * jnp.sum(xf * xf, axis=1)
    row_basket = jnp.sum(xf * basket[None, :], axis=1)
    return query, row_term, row_basket


def prepare_cols(y_cols, basket):
    yf = y_cols.astype(jnp.float32)
    width = yf.shape[1]
    col_term = -(KAPPA / width) * jnp.sum(yf * yf, axis=1)
    col_basket = jnp.sum(yf * basket[None, :], axis=1)
    features = jnp.concatenate([yf, yf * yf], axis=1).astype(jnp.bfloat16)
    return yf, col_term, col_basket, features


def scores(query, row_term, row_basket, y_float, col_term, col_basket):
    dots = lax.dot_general(query, y_float, (((1,), (1,)), ((), ())), precision=lax.Precision.HIGHEST, preferred_element_type=jnp.float32)
    payoff = jax.nn.relu(col_basket[None, :] - row_basket[:, None])
    return (dots + row_term[:, None] + col_term[None, :] + payoff) / EPS


def reference(x_points, y_points, row_mass, col_mass, multipliers, col_potential, basket, damping):
    query, row_term, row_basket = prepare_rows(x_points, multipliers, basket)
    y_float, col_term, col_basket, features = prepare_cols(y_points, basket)
    row_weight = row_mass.astype(jnp.float32)
    col_weight = col_mass.astype(jnp.float32)
    log_mu = jnp.log(row_weight) - jnp.log(jnp.sum(row_weight))
    log_nu = jnp.log(col_weight) - jnp.log(jnp.sum(col_weight))
    block = min(128, NX)
    count = NX // block
    starts = jnp.arange(count, dtype=jnp.int32) * block
    gshift = col_potential.astype(jnp.float32) / EPS + log_nu

    def cut(arr, start):
        return lax.dynamic_slice_in_dim(arr, start.astype(jnp.int32), block, 0)

    def block_scores(start):
        return scores(cut(query, start), cut(row_term, start), cut(row_basket, start), y_float, col_term, col_basket)

    def row_pass(start):
        z = block_scores(start) + gshift[None, :]
        top = jnp.max(z, axis=1)
        total = jnp.sum(jnp.exp(z - top[:, None]), axis=1)
        return top + jnp.log(total)

    row_potential = -EPS * lax.map(row_pass, starts).reshape(NX)
    fshift = row_potential / EPS + log_mu

    def col_pass(start):
        z = block_scores(start) + cut(fshift, start)[:, None]
        top = jnp.max(z, axis=0)
        total = jnp.sum(jnp.exp(z - top[None, :]), axis=0)
        return top, total

    tops, totals = lax.map(col_pass, starts)
    top = jnp.max(tops, axis=0)
    total = jnp.sum(totals * jnp.exp(tops - top[None, :]), axis=0)
    col_potential_new = -EPS * (top + jnp.log(total))
    gq = col_potential_new / EPS + log_nu
    fq = row_potential / EPS

    def moment_pass(start):
        plan = jnp.exp(block_scores(start) + cut(fq, start)[:, None] + gq[None, :]).astype(jnp.bfloat16)
        both = jnp.dot(plan, features, preferred_element_type=jnp.float32)
        mass = jnp.sum(plan.astype(jnp.float32), axis=1)
        return both, mass

    both, mass = lax.map(moment_pass, starts)
    both = both.reshape(NX, 2 * A)
    mass = mass.reshape(NX)
    first = both[:, :A]
    second = both[:, A:]
    xf = x_points.astype(jnp.float32)
    grad = first - xf * mass[:, None]
    curv = (second - 2.0 * xf * first + xf * xf * mass[:, None]) / EPS + RIDGE
    multipliers_new = multipliers.astype(jnp.float32) - damping[None, :] * grad / curv
    return row_potential, col_potential_new, multipliers_new
```

```python
import functools
import math
import jax
import jax.numpy as jnp
from jax import lax
from jax.experimental import pallas as pl
from jax.experimental.pallas import tpu as pltpu
from jax.sharding import PartitionSpec as P

EPS = 0.5
KAPPA = 0.5
RIDGE = 1.0
L2E = math.log2(math.e)
LN2 = math.log(2.0)
SCALE = L2E / EPS
LOW = -1e30
F32 = jnp.float32
BF16 = jnp.bfloat16


def split3(value):
    one = value.astype(BF16).astype(F32)
    rest = value - one
    two = rest.astype(BF16).astype(F32)
    return one, two, rest - two


def log2(value):
    return jnp.log(value) * L2E


def kernel(
    nrow, ncol,
    xm_ref, rmass_ref, yt_ref, cinfo_ref, basket_ref, damping_ref,
    rowpot_ref, colpot_ref, mult_ref,
    xbuf, rbuf, ybuf, cbuf, rowmsg, colout, colmsg, cpbuf, gout, gbuf, mout, mbuf,
    q_s, q3_s, rt_s, rb_s, y_s, ft_s, cb_s, ct_s, top_s, sum_s, z_s, plan_s, g_s, f_s,
    xsend, xrecv, rsend, rrecv, zsend, wsend, yrecv, czsend, cwsend, crecv,
    rmsend, rmrecv, cmsend, cmrecv, cpsend, cprecv, gsend, grecv, msend, mrecv,
):
    r = lax.axis_index("row")
    c = lax.axis_index("col")
    xs = xm_ref.shape[0]
    cb = yt_ref.shape[1]
    width = yt_ref.shape[0]
    rows = xs * ncol
    half = nrow // 2
    pair = r % 2
    group = r // 2
    twin = r + 1 - 2 * pair

    def to_col(src, dst, send, recv, other):
        return pltpu.make_async_remote_copy(
            src_ref=src, dst_ref=dst, send_sem=send, recv_sem=recv,
            device_id=(r, other), device_id_type=pl.DeviceIdType.MESH)

    def to_row(src, dst, send, recv, other):
        return pltpu.make_async_remote_copy(
            src_ref=src, dst_ref=dst, send_sem=send, recv_sem=recv,
            device_id=(other, c), device_id_type=pl.DeviceIdType.MESH)

    barrier = pltpu.get_barrier_semaphore()

    @pl.loop(1, ncol)
    def _(k):
        pl.semaphore_signal(barrier, inc=1, device_id=(r, (c + k) % ncol),
                            device_id_type=pl.DeviceIdType.MESH)

    @pl.loop(1, nrow)
    def _(k):
        pl.semaphore_signal(barrier, inc=1, device_id=((r + k) % nrow, c),
                            device_id_type=pl.DeviceIdType.MESH)

    xbuf[c] = xm_ref[...]
    rbuf[c] = rmass_ref[...]
    ybuf[r] = yt_ref[...]
    cbuf[r] = cinfo_ref[...]
    pl.semaphore_wait(barrier, nrow + ncol - 2)

    def x_copy(k, owner):
        return to_col(xbuf.at[owner], xbuf.at[owner], xsend.at[k], xrecv.at[owner],
                      (c + k) % ncol)

    def r_copy(k, owner):
        return to_col(rbuf.at[owner], rbuf.at[owner], rsend.at[k], rrecv.at[owner],
                      (c + k) % ncol)

    @pl.loop(1, ncol)
    def _(k):
        x_copy(k, c).start()
        r_copy(k, c).start()

    def same(k):
        return ((group + half - k) % half) * 2 + pair

    def other(k):
        return ((group + half - k) % half) * 2 + 1 - pair

    def z_copies(k, block):
        goal = ((group + k) % half) * 2 + pair
        return (to_row(cbuf.at[block], cbuf.at[block], czsend.at[k], crecv.at[block], goal),
                to_row(ybuf.at[block], ybuf.at[block], zsend.at[k], yrecv.at[block], goal))

    def w_copies(k, block):
        return (to_row(cbuf.at[block], cbuf.at[block], cwsend.at[k], crecv.at[block], twin),
                to_row(ybuf.at[block], ybuf.at[block], wsend.at[k], yrecv.at[block], twin))

    for copy in w_copies(0, r):
        copy.start()

    @pl.loop(1, half)
    def _(k):
        for copy in z_copies(k, r):
            copy.start()

    top_s[...] = jnp.full(top_s.shape, LOW, F32)
    sum_s[...] = jnp.zeros(sum_s.shape, F32)

    def prepare_block(b):
        y16 = ybuf[b]
        yf = y16.astype(F32)
        sq = yf * yf
        y_s[b, 0:width] = y16
        y_s[b, width:2 * width] = y16
        y_s[b, 2 * width:3 * width] = y16
        y_s[b, 3 * width:4 * width] = jnp.zeros((width, cb), BF16)
        ft_s[b, 0:width] = y16
        ft_s[b, width:2 * width] = sq.astype(BF16)
        ones = lax.broadcasted_iota(jnp.int32, (2 * width, cb), 0) == 0
        ft_s[b, 2 * width:4 * width] = jnp.where(ones, 1.0, 0.0).astype(BF16)
        ct_s[b] = -(SCALE * KAPPA / width) * jnp.sum(sq, axis=0, keepdims=True)
        basket = SCALE * jnp.sum(yf * basket_ref[1][0:width, 0:1], axis=0, keepdims=True)
        cb_s[b] = jnp.broadcast_to(basket, (8, cb))

    def put_cols(b, value):
        row = lax.broadcasted_iota(jnp.int32, (16, cb), 0)
        one, two, three = split3(value)
        ext = jnp.where(row < 3, 1.0, 0.0)
        ext = jnp.where(row == 3, one, ext)
        ext = jnp.where(row == 4, two, ext)
        ext = jnp.where(row == 5, three, ext)
        y_s[b, 3 * width:3 * width + 16] = ext.astype(BF16)

    def put_rows(start, size, value):
        lane = lax.broadcasted_iota(jnp.int32, (size, 128), 1)
        one, two, three = split3(value)
        ext = jnp.where((lane >= 67) & (lane < 70), 1.0, q3_s[pl.ds(start, size)])
        ext = jnp.where(lane == 64, one, ext)
        ext = jnp.where(lane == 65, two, ext)
        ext = jnp.where(lane == 66, three, ext)
        q_s[pl.ds(start, size), 128:256] = ext.astype(BF16)

    prepare_block(r)

    @pl.loop(1, ncol)
    def _(k):
        owner = (c + ncol - k) % ncol
        x_copy(k, owner).wait_recv()
        r_copy(k, owner).wait_recv()

    @pl.loop(0, ncol)
    def _(k):
        both = xbuf[k].astype(F32)
        x = both[:, 0:128]
        h = both[:, 128:256]
        lane = lax.broadcasted_iota(jnp.int32, (xs, 128), 1)
        one, two, three = split3(SCALE * (h + (2.0 * KAPPA / width) * x))
        here = pl.ds(k * xs, xs)
        xb = x * basket_ref[0][0:1, :]
        q_s[here, 0:128] = jnp.where(lane < 64, one, two).astype(BF16)
        q3_s[here] = jnp.where(lane < 64, three, 0.0)
        term = -0.5 * (h * x + (KAPPA / width) * (x * x)) - xb
        rt = jnp.broadcast_to(SCALE * jnp.sum(term, axis=1, keepdims=True), (xs, 128))
        rb_s[here] = jnp.broadcast_to(SCALE * jnp.sum(xb, axis=1, keepdims=True), (xs, 128))
        rt_s[here] = rt
        put_rows(k * xs, xs, rt)

    chunk = min(256, rows)
    tiles = cb // 128

    def dots(b):
        for start in range(0, rows, chunk):
            z_s[start:start + chunk] = jnp.dot(
                q_s[start:start + chunk], y_s[b], preferred_element_type=F32)

    def row_block(b):
        put_cols(b, ct_s[b] + cbuf[b, 0:1])
        dots(b)
        size = 32

        def step(i, _):
            here = pl.ds(pl.multiple_of(i * size, size), size)
            rb = rb_s[here]
            vals = []
            for t in range(tiles):
                span = slice(t * 128, (t + 1) * 128)
                vals.append(z_s[here, span] + jnp.maximum(cb_s[b, 0:1, span], rb))
            old = top_s[here]
            top = functools.reduce(jnp.maximum, vals, old)
            total = sum_s[here] * jnp.exp2(old - top)
            for val in vals:
                total = total + jnp.exp2(val - top)
            top_s[here] = top
            sum_s[here] = total
            return 0

        lax.fori_loop(0, rows // size, step, 0, unroll=True)

    @pl.loop(0, half)
    def _(k):
        first = same(k)

        @pl.when(k > 0)
        def _():
            for copy in z_copies(k, first):
                copy.wait_recv()
            for copy in w_copies(k, first):
                copy.start()
            prepare_block(first)

        row_block(first)
        second = other(k)
        for copy in w_copies(k, second):
            copy.wait_recv()
        prepare_block(second)
        row_block(second)

    tops = top_s[...].T
    sums = sum_s[...].T
    top = jnp.max(tops, axis=0, keepdims=True)
    total = jnp.sum(sums * jnp.exp2(tops - top), axis=0, keepdims=True)
    nu_part = cbuf[0, 1:2]
    for b in range(1, nrow):
        nu_part = nu_part + cbuf[b, 1:2]
    nu_part = jnp.sum(nu_part, axis=1, keepdims=True)
    rowmsg[c, 0:1] = top
    rowmsg[c, 1:2] = total
    rowmsg[c, 2:3] = jnp.broadcast_to(nu_part, (1, rows))
    rowmsg[c, 3:4] = jnp.zeros((1, rows), F32)

    def rm_copy(k, owner):
        return to_col(rowmsg.at[owner], rowmsg.at[owner], rmsend.at[k], rmrecv.at[owner],
                      (c + k) % ncol)

    @pl.loop(1, ncol)
    def _(k):
        rm_copy(k, c).start()

    @pl.loop(1, ncol)
    def _(k):
        rm_copy(k, (c + ncol - k) % ncol).wait_recv()

    top = functools.reduce(jnp.maximum, [rowmsg[k, 0:1] for k in range(ncol)])
    total = sum(rowmsg[k, 1:2] * jnp.exp2(rowmsg[k, 0:1] - top) for k in range(ncol))
    nu_log = log2(sum(rowmsg[k, 2:3] for k in range(ncol)))
    f_row = nu_log - (top + log2(total))
    rowpot_ref[...] = (EPS * LN2) * f_row
    nu_col = jnp.broadcast_to(nu_log[:, 0:1], (1, cb))
    masses = jnp.concatenate([rbuf[k] for k in range(ncol)], axis=1)
    mu_part = jnp.broadcast_to(jnp.sum(masses, axis=1, keepdims=True), (1, cb))
    f_s[...] = rt_s[...] + jnp.broadcast_to(f_row, (128, rows)).T
    shifted = rt_s[...] + jnp.broadcast_to(f_row + log2(masses), (128, rows)).T
    put_rows(0, rows, shifted)

    def cm_copy(k, block, owner):
        return to_row(colout.at[block], colmsg.at[owner], cmsend.at[k], cmrecv.at[owner],
                      (r + k) % nrow)

    size = 64
    span_cols = min(512, cb)

    @pl.loop(0, nrow)
    def _(k):
        b = (r + 1 + k) % nrow
        put_cols(b, ct_s[b])
        dots(b)
        for span_start in range(0, cb, span_cols):
            span = slice(span_start, span_start + span_cols)
            lo = cb_s[b, :, span]

            def step(i, carry):
                old, total = carry
                vals = []
                for t in range(size // 8):
                    here = pl.ds(pl.multiple_of(i * size + t * 8, 8), 8)
                    rb = rb_s[here]
                    wide = jnp.concatenate([rb] * (span_cols // 128), axis=1)
                    vals.append(z_s[here, span] + jnp.maximum(lo, wide))
                top = functools.reduce(jnp.maximum, vals, old)
                total = total * jnp.exp2(old - top)
                for val in vals:
                    total = total + jnp.exp2(val - top)
                return top, total

            tops, sums = lax.fori_loop(
                0, rows // size, step,
                (jnp.full((8, span_cols), LOW, F32), jnp.zeros((8, span_cols), F32)),
                unroll=True)
            top = jnp.max(tops, axis=0, keepdims=True)
            colout[b, 0:1, span] = top
            colout[b, 1:2, span] = jnp.sum(sums * jnp.exp2(tops - top), axis=0, keepdims=True)
        colout[b, 2:3] = mu_part
        colout[b, 3:4] = jnp.zeros((1, cb), F32)

        @pl.when(k < nrow - 1)
        def _():
            cm_copy(k + 1, b, r).start()

    colmsg[r] = colout[r]
    put_rows(0, rows, f_s[...])

    @pl.loop(1, nrow)
    def _(k):
        cm_copy(k, r, (r + nrow - k) % nrow).wait_recv()

    top = functools.reduce(jnp.maximum, [colmsg[k, 0:1] for k in range(nrow)])
    total = sum(colmsg[k, 1:2] * jnp.exp2(colmsg[k, 0:1] - top) for k in range(nrow))
    mu_log = log2(sum(colmsg[k, 2:3] for k in range(nrow)))
    cpbuf[r] = (EPS * LN2) * (mu_log - (top + log2(total)))

    def cp_copy(k, owner):
        return to_row(cpbuf.at[owner], cpbuf.at[owner], cpsend.at[k], cprecv.at[owner],
                      (r + k) % nrow)

    @pl.loop(1, nrow)
    def _(k):
        cp_copy(k, r).start()

    g_s[...] = jnp.zeros(g_s.shape, F32)

    def g_copy(k, chunk_id, owner):
        return to_col(gout.at[chunk_id], gbuf.at[owner], gsend.at[k], grecv.at[owner],
                      (c + k) % ncol)

    def m_copy(k, chunk_id, owner):
        return to_col(mout.at[chunk_id], mbuf.at[owner], msend.at[k], mrecv.at[owner],
                      (c + k) % ncol)

    sub = min(256, cb)

    @pl.loop(0, ncol)
    def _(s):
        q = (c + ncol - 1 - s) % ncol
        base = pl.multiple_of(q * xs, xs)

        @pl.loop(0, nrow)
        def _(k):
            b = (r + nrow - k) % nrow

            @pl.when(s == 0)
            def _():
                @pl.when(k > 0)
                def _():
                    cp_copy(k, b).wait_recv()

                put_cols(b, ct_s[b] + (1.0 / (EPS * LN2)) * cpbuf[b]
                         + log2(cbuf[b, 1:2]) - nu_col)

            qq = q_s[pl.ds(base, xs)]
            acc = g_s[pl.ds(base, xs)]
            for start in range(0, cb, sub):
                cols = slice(start, start + sub)
                z = jnp.dot(qq, y_s[b, :, cols], preferred_element_type=F32)
                rb = rb_s[pl.ds(base, xs)]
                parts = []
                for t in range(0, sub, 128):
                    val = z[:, t:t + 128] + jnp.maximum(
                        cb_s[b, 0:1, start + t:start + t + 128], rb)
                    parts.append(jnp.exp2(val).astype(BF16))
                plan = jnp.concatenate(parts, axis=1)
                acc = acc + lax.dot_general(
                    plan, ft_s[b, :, cols], (((1,), (1,)), ((), ())),
                    preferred_element_type=F32)
            g_s[pl.ds(base, xs)] = acc

        gout[q] = g_s[pl.ds(base, xs), 0:128]
        mout[q] = g_s[pl.ds(base, xs), 128:256].T[0:8]

        @pl.when(s < ncol - 1)
        def _():
            g_copy(ncol - 1 - s, q, c).start()
            m_copy(ncol - 1 - s, q, c).start()

    for b in range(nrow):
        colpot_ref[b] = cpbuf[b]

    gbuf[c] = gout[c]
    mbuf[c] = mout[c]

    @pl.loop(1, ncol)
    def _(k):
        owner = (c + ncol - k) % ncol
        g_copy(k, c, owner).wait_recv()
        m_copy(k, c, owner).wait_recv()

    moments = sum(gbuf[k] for k in range(ncol))
    mass_row = sum(mbuf[k] for k in range(ncol))[0:1]
    mass = jnp.broadcast_to(mass_row, (128, xs)).T
    both = xm_ref[...].astype(F32)
    x = both[:, 0:128]
    h = both[:, 128:256]
    second = pltpu.roll(moments, 64, 1)
    grad = moments - x * mass
    curv = (second - 2.0 * x * moments + x * x * mass) / EPS + RIDGE
    new = h - damping_ref[...] * grad / curv
    mult_ref[...] = new[:, 0:width]

    @pl.loop(1, ncol)
    def _(k):
        x_copy(k, c).wait_send()
        r_copy(k, c).wait_send()
        rm_copy(k, c).wait_send()
        g_copy(k, (c + k) % ncol, c).wait_send()
        m_copy(k, (c + k) % ncol, c).wait_send()

    @pl.loop(1, nrow)
    def _(k):
        cm_copy(k, (r + k) % nrow, r).wait_send()
        cp_copy(k, r).wait_send()

    @pl.loop(0, half)
    def _(k):
        for copy in w_copies(k, same(k)):
            copy.wait_send()

    @pl.loop(1, half)
    def _(k):
        for copy in z_copies(k, r):
            copy.wait_send()


def on_device(nrow, ncol, x_points, y_points, row_mass, col_mass, multipliers, col_potential,
              basket, damping):
    xs, width = x_points.shape
    cb = y_points.shape[0]
    rows = xs * ncol
    xm = jnp.concatenate([x_points, x_points, multipliers, multipliers], axis=1)
    rmass = row_mass.astype(F32)[None, :]
    cmass = col_mass.astype(F32)
    cinfo = jnp.stack([SCALE * col_potential.astype(F32) + L2E * jnp.log(cmass), cmass])
    lanes = jnp.concatenate([basket, jnp.zeros((128 - width,), F32)])
    baskets = jnp.stack([jnp.broadcast_to(lanes[None, :], (128, 128)),
                         jnp.broadcast_to(lanes[:, None], (128, 128))])
    damp = jnp.concatenate([damping, damping])[None, :]
    half = nrow // 2
    dma = pltpu.SemaphoreType.DMA
    vmem = pltpu.VMEM
    whole = pl.BlockSpec(memory_space=pltpu.VMEM)
    row_pot, col_pot, mult = pl.pallas_call(
        functools.partial(kernel, nrow, ncol),
        out_shape=(jax.ShapeDtypeStruct((1, rows), F32),
                   jax.ShapeDtypeStruct((nrow, 1, cb), F32),
                   jax.ShapeDtypeStruct((xs, width), F32)),
        in_specs=[whole] * 6,
        out_specs=(whole,) * 3,
        scratch_shapes=[
            vmem((ncol, xs, 256), BF16), vmem((ncol, 1, xs), F32),
            vmem((nrow, width, cb), BF16), vmem((nrow, 2, cb), F32),
            vmem((ncol, 4, rows), F32), vmem((nrow, 4, cb), F32), vmem((nrow, 4, cb), F32),
            vmem((nrow, 1, cb), F32),
            vmem((ncol, xs, 128), F32), vmem((ncol, xs, 128), F32),
            vmem((ncol, 8, xs), F32), vmem((ncol, 8, xs), F32),
            vmem((rows, 256), BF16), vmem((rows, 128), F32), vmem((rows, 128), F32),
            vmem((rows, 128), F32), vmem((nrow, 256, cb), BF16), vmem((nrow, 256, cb), BF16),
            vmem((nrow, 8, cb), F32), vmem((nrow, 1, cb), F32),
            vmem((rows, 128), F32), vmem((rows, 128), F32), vmem((rows, cb), F32),
            vmem((8, 128), BF16), vmem((rows, 256), F32), vmem((rows, 128), F32),
            dma((ncol,)), dma((ncol,)), dma((ncol,)), dma((ncol,)),
            dma((half,)), dma((half,)), dma((nrow,)),
            dma((half,)), dma((half,)), dma((nrow,)),
            dma((ncol,)), dma((ncol,)), dma((nrow,)), dma((nrow,)),
            dma((nrow,)), dma((nrow,)), dma((ncol,)), dma((ncol,)),
            dma((ncol,)), dma((ncol,)),
        ],
        compiler_params=pltpu.CompilerParams(
            collective_id=0, has_side_effects=True, vmem_limit_bytes=56 * 1024 * 1024),
    )(xm, rmass, y_points.T, cinfo, baskets, damp)
    return row_pot.reshape(rows), col_pot.reshape(nrow * cb), mult


def solution(mesh):
    placed = (
        P(("row", "col"), None),
        P(("col", "row"), None),
        P(("row", "col")),
        P(("col", "row")),
        P(("row", "col"), None),
        P(("col", "row")),
        P(),
        P(),
    )
    return jax.shard_map(
        functools.partial(on_device, mesh.shape["row"], mesh.shape["col"]),
        mesh=mesh,
        in_specs=placed,
        out_specs=(P("row"), P("col"), P(("row", "col"), None)),
        check_vma=False,
    )
```

```python
import functools
import math
import jax
import jax.numpy as jnp
from jax import lax
from jax.experimental import pallas as pl
from jax.experimental.pallas import tpu as pltpu
from jax.sharding import PartitionSpec as P

EPS = 0.5
KAPPA = 0.5
RIDGE = 1.0
L2E = math.log2(math.e)
LN2 = math.log(2.0)
SCALE = L2E / EPS
LOW = -1e30
F32 = jnp.float32
BF16 = jnp.bfloat16


def split3(value):
    one = value.astype(BF16).astype(F32)
    rest = value - one
    two = rest.astype(BF16).astype(F32)
    return one, two, rest - two


def log2(value):
    return jnp.log(value) * L2E


def kernel(
    nrow, ncol,
    xt_ref, mt_ref, rmass_ref, yt_ref, pot_ref, cmass_ref, basket_ref, damping_ref,
    rowpot_ref, colpot_ref, mult_ref,
    xbuf, rbuf, ybuf, cbuf, rowmsg, colout, colmsg, cpbuf, gout, gbuf, mout, mbuf,
    q_s, q3_s, rt_s, rb_s, y_s, ft_s, cb_s, ct_s, top_s, sum_s, za_s, zb_s, bc_s, g_s, f_s,
    xsend, xrecv, rsend, rrecv, zsend, wsend, yrecv, czsend, cwsend, crecv,
    rmsend, rmrecv, cmsend, cmrecv, cpsend, cprecv, gsend, grecv, msend, mrecv,
):
    r = lax.axis_index("row")
    c = lax.axis_index("col")
    xs = xt_ref.shape[1]
    cb = yt_ref.shape[1]
    width = yt_ref.shape[0]
    rows = xs * ncol
    half = nrow // 2
    pair = r % 2
    group = r // 2
    twin = r + 1 - 2 * pair

    def to_col(src, dst, send, recv, other):
        return pltpu.make_async_remote_copy(
            src_ref=src, dst_ref=dst, send_sem=send, recv_sem=recv,
            device_id=(r, other), device_id_type=pl.DeviceIdType.MESH)

    def to_row(src, dst, send, recv, other):
        return pltpu.make_async_remote_copy(
            src_ref=src, dst_ref=dst, send_sem=send, recv_sem=recv,
            device_id=(other, c), device_id_type=pl.DeviceIdType.MESH)

    barrier = pltpu.get_barrier_semaphore()

    @pl.loop(1, ncol)
    def _(k):
        pl.semaphore_signal(barrier, inc=1, device_id=(r, (c + k) % ncol),
                            device_id_type=pl.DeviceIdType.MESH)

    @pl.loop(1, nrow)
    def _(k):
        pl.semaphore_signal(barrier, inc=1, device_id=((r + k) % nrow, c),
                            device_id_type=pl.DeviceIdType.MESH)

    xbuf[c] = jnp.concatenate([xt_ref[...], mt_ref[...]], axis=0).astype(F32).T.astype(BF16)
    rbuf[c] = rmass_ref[...]
    ybuf[r] = yt_ref[...]
    cbuf[r, 0:1] = SCALE * pot_ref[...] + log2(cmass_ref[...])
    cbuf[r, 1:2] = cmass_ref[...]
    basket_row = jnp.concatenate([basket_ref[...], jnp.zeros((1, 128 - width), F32)], axis=1)
    pl.semaphore_wait(barrier, nrow + ncol - 2)

    def x_copy(k, owner):
        return to_col(xbuf.at[owner], xbuf.at[owner], xsend.at[k], xrecv.at[owner],
                      (c + k) % ncol)

    def r_copy(k, owner):
        return to_col(rbuf.at[owner], rbuf.at[owner], rsend.at[k], rrecv.at[owner],
                      (c + k) % ncol)

    @pl.loop(1, ncol)
    def _(k):
        x_copy(k, c).start()
        r_copy(k, c).start()

    def same(k):
        return ((group + 2 * half - k) % half) * 2 + pair

    def other(k):
        return ((group + half - k) % half) * 2 + 1 - pair

    def z_copies(k, block):
        goal = ((group + k) % half) * 2 + pair
        return (to_row(cbuf.at[block], cbuf.at[block], czsend.at[k], crecv.at[block], goal),
                to_row(ybuf.at[block], ybuf.at[block], zsend.at[k], yrecv.at[block], goal))

    def w_copies(k, block):
        return (to_row(cbuf.at[block], cbuf.at[block], cwsend.at[k], crecv.at[block], twin),
                to_row(ybuf.at[block], ybuf.at[block], wsend.at[k], yrecv.at[block], twin))

    for copy in w_copies(0, r):
        copy.start()

    @pl.loop(1, half)
    def _(k):
        for copy in z_copies(k, r):
            copy.start()

    bc_s[...] = jnp.broadcast_to(basket_row, (128, 128)).T
    one_lane = lax.broadcasted_iota(jnp.int32, (cb, 128), 1) == 0
    ones = jnp.where(one_lane, 1.0, 0.0).astype(BF16)

    @pl.loop(0, nrow)
    def _(b):
        y_s[b, 3 * width:4 * width] = jnp.zeros((width, cb), BF16)
        ft_s[b, :, 128:256] = ones

    top_s[...] = jnp.full(top_s.shape, LOW, F32)
    sum_s[...] = jnp.zeros(sum_s.shape, F32)

    def prepare_block(b):
        y16 = ybuf[b]
        yf = y16.astype(F32)
        sq = yf * yf
        y_s[b, 0:width] = y16
        y_s[b, width:2 * width] = y16
        y_s[b, 2 * width:3 * width] = y16
        ft_s[b, :, 0:128] = jnp.concatenate([yf, sq], axis=0).T.astype(BF16)
        ct_s[b] = -(SCALE * KAPPA / width) * jnp.sum(sq, axis=0, keepdims=True)
        wide = jnp.concatenate([bc_s[0:width]] * (cb // 128), axis=1)
        basket = SCALE * jnp.sum(yf * wide, axis=0, keepdims=True)
        cb_s[b] = jnp.broadcast_to(basket, (8, cb))

    def doubled(both, lane):
        both = both.astype(F32)
        swapped = pltpu.roll(both, 64, 1)
        return jnp.where(lane < 64, both, swapped), jnp.where(lane < 64, swapped, both)

    def put_cols(b, value):
        row = lax.broadcasted_iota(jnp.int32, (16, cb), 0)
        one, two, three = split3(value)
        ext = jnp.where(row < 3, 1.0, 0.0)
        ext = jnp.where(row == 3, one, ext)
        ext = jnp.where(row == 4, two, ext)
        ext = jnp.where(row == 5, three, ext)
        y_s[b, 3 * width:3 * width + 16] = ext.astype(BF16)

    def put_rows(start, size, value):
        lane = lax.broadcasted_iota(jnp.int32, (size, 128), 1)
        one, two, three = split3(value)
        ext = jnp.where((lane >= 67) & (lane < 70), 1.0, q3_s[pl.ds(start, size)])
        ext = jnp.where(lane == 64, one, ext)
        ext = jnp.where(lane == 65, two, ext)
        ext = jnp.where(lane == 66, three, ext)
        q_s[pl.ds(start, size), 128:256] = ext.astype(BF16)

    prepare_block(r)

    @pl.loop(1, ncol)
    def _(k):
        owner = (c + ncol - k) % ncol
        x_copy(k, owner).wait_recv()
        r_copy(k, owner).wait_recv()

    @pl.loop(0, ncol)
    def _(k):
        lane = lax.broadcasted_iota(jnp.int32, (xs, 128), 1)
        x, h = doubled(xbuf[k], lane)
        one, two, three = split3(SCALE * (h + (2.0 * KAPPA / width) * x))
        here = pl.ds(k * xs, xs)
        xb = x * basket_row
        q_s[here, 0:128] = jnp.where(lane < 64, one, two).astype(BF16)
        q3_s[here] = jnp.where(lane < 64, three, 0.0)
        term = -0.5 * (h * x + (KAPPA / width) * (x * x)) - xb
        rt = jnp.broadcast_to(SCALE * jnp.sum(term, axis=1, keepdims=True), (xs, 128))
        rb_s[here] = jnp.broadcast_to(SCALE * jnp.sum(xb, axis=1, keepdims=True), (xs, 128))
        rt_s[here] = rt
        put_rows(k * xs, xs, rt)

    chunk = min(256, cb)
    tiles = cb // 128

    def dots(b, z_s):
        for start in range(0, cb, chunk):
            cols = slice(start, start + chunk)
            z_s[:, cols] = jnp.dot(q_s[...], y_s[b, :, cols], preferred_element_type=F32)

    def row_dots(b, z_s):
        put_cols(b, ct_s[b] + cbuf[b, 0:1])
        dots(b, z_s)

    def row_block(b, z_s):
        size = 32

        def step(i, _):
            here = pl.ds(pl.multiple_of(i * size, size), size)
            rb = rb_s[here]
            vals = []
            for t in range(tiles):
                span = slice(t * 128, (t + 1) * 128)
                vals.append(z_s[here, span] + jnp.maximum(cb_s[b, 0:1, span], rb))
            old = top_s[here]
            top = functools.reduce(jnp.maximum, vals, old)
            total = sum_s[here] * jnp.exp2(old - top)
            for val in vals:
                total = total + jnp.exp2(val - top)
            top_s[here] = top
            sum_s[here] = total
            return 0

        lax.fori_loop(0, rows // size, step, 0, unroll=True)

    row_dots(r, za_s)

    @pl.loop(0, half)
    def _(k):
        first = same(k)
        second = other(k)
        for copy in w_copies(k, second):
            copy.wait_recv()
        prepare_block(second)
        row_dots(second, zb_s)
        row_block(first, za_s)
        later = same(k + 1)

        @pl.when(k < half - 1)
        def _():
            for copy in z_copies(k + 1, later):
                copy.wait_recv()
            for copy in w_copies(k + 1, later):
                copy.start()
            prepare_block(later)

        row_dots(later, za_s)
        row_block(second, zb_s)

    tops = top_s[...].T
    sums = sum_s[...].T
    top = jnp.max(tops, axis=0, keepdims=True)
    total = jnp.sum(sums * jnp.exp2(tops - top), axis=0, keepdims=True)
    nu_part = cbuf[0, 1:2]
    for b in range(1, nrow):
        nu_part = nu_part + cbuf[b, 1:2]
    nu_part = jnp.sum(nu_part, axis=1, keepdims=True)
    rowmsg[c, 0:1] = top
    rowmsg[c, 1:2] = total
    rowmsg[c, 2:3] = jnp.broadcast_to(nu_part, (1, rows))
    rowmsg[c, 3:4] = jnp.zeros((1, rows), F32)

    def rm_copy(k, owner):
        return to_col(rowmsg.at[owner], rowmsg.at[owner], rmsend.at[k], rmrecv.at[owner],
                      (c + k) % ncol)

    @pl.loop(1, ncol)
    def _(k):
        rm_copy(k, c).start()

    masses = jnp.concatenate([rbuf[k] for k in range(ncol)], axis=1)
    mu_part = jnp.broadcast_to(jnp.sum(masses, axis=1, keepdims=True), (1, cb))
    top_s[...] = rt_s[...] + jnp.broadcast_to(log2(masses), (128, rows)).T

    @pl.loop(1, ncol)
    def _(k):
        rm_copy(k, (c + ncol - k) % ncol).wait_recv()

    top = functools.reduce(jnp.maximum, [rowmsg[k, 0:1] for k in range(ncol)])
    total = sum(rowmsg[k, 1:2] * jnp.exp2(rowmsg[k, 0:1] - top) for k in range(ncol))
    nu_log = log2(sum(rowmsg[k, 2:3] for k in range(ncol)))
    f_row = nu_log - (top + log2(total))
    rowpot_ref[...] = (EPS * LN2) * f_row
    nu_col = jnp.broadcast_to(nu_log[:, 0:1], (1, cb))
    f_col = jnp.broadcast_to(f_row, (128, rows)).T
    f_s[...] = rt_s[...] + f_col
    put_rows(0, rows, top_s[...] + f_col)

    def cm_copy(k, block, owner):
        return to_row(colout.at[block], colmsg.at[owner], cmsend.at[k], cmrecv.at[owner],
                      (r + k) % nrow)

    size = 64
    span_cols = min(512, cb)

    def col_dots(k, z_s):
        b = (r + 1 + k) % nrow
        put_cols(b, ct_s[b])
        dots(b, z_s)

    def col_block(k, z_s):
        b = (r + 1 + k) % nrow
        for span_start in range(0, cb, span_cols):
            span = slice(span_start, span_start + span_cols)
            lo = cb_s[b, :, span]

            def step(i, carry):
                old, total = carry
                vals = []
                for t in range(size // 8):
                    here = pl.ds(pl.multiple_of(i * size + t * 8, 8), 8)
                    rb = rb_s[here]
                    wide = jnp.concatenate([rb] * (span_cols // 128), axis=1)
                    vals.append(z_s[here, span] + jnp.maximum(lo, wide))
                top = functools.reduce(jnp.maximum, vals, old)
                total = total * jnp.exp2(old - top)
                for val in vals:
                    total = total + jnp.exp2(val - top)
                return top, total

            tops, sums = lax.fori_loop(
                0, rows // size, step,
                (jnp.full((8, span_cols), LOW, F32), jnp.zeros((8, span_cols), F32)),
                unroll=True)
            top = jnp.max(tops, axis=0, keepdims=True)
            colout[b, 0:1, span] = top
            colout[b, 1:2, span] = jnp.sum(sums * jnp.exp2(tops - top), axis=0, keepdims=True)
        colout[b, 2:3] = mu_part
        colout[b, 3:4] = jnp.zeros((1, cb), F32)

        @pl.when(k < nrow - 1)
        def _():
            cm_copy(k + 1, b, r).start()

    col_dots(0, za_s)

    @pl.loop(0, half)
    def _(j):
        col_dots(2 * j + 1, zb_s)
        col_block(2 * j, za_s)
        col_dots(2 * j + 2, za_s)
        col_block(2 * j + 1, zb_s)

    colmsg[r] = colout[r]
    put_rows(0, rows, f_s[...])

    @pl.loop(1, nrow)
    def _(k):
        cm_copy(k, r, (r + nrow - k) % nrow).wait_recv()

    top = functools.reduce(jnp.maximum, [colmsg[k, 0:1] for k in range(nrow)])
    total = sum(colmsg[k, 1:2] * jnp.exp2(colmsg[k, 0:1] - top) for k in range(nrow))
    mu_log = log2(sum(colmsg[k, 2:3] for k in range(nrow)))
    cpbuf[r] = (EPS * LN2) * (mu_log - (top + log2(total)))

    def cp_copy(k, owner):
        return to_row(cpbuf.at[owner], cpbuf.at[owner], cpsend.at[k], cprecv.at[owner],
                      (r + k) % nrow)

    @pl.loop(1, nrow)
    def _(k):
        cp_copy(k, r).start()

    g_s[...] = jnp.zeros(g_s.shape, F32)

    def g_copy(k, chunk_id, owner):
        return to_col(gout.at[chunk_id], gbuf.at[owner], gsend.at[k], grecv.at[owner],
                      (c + k) % ncol)

    def m_copy(k, chunk_id, owner):
        return to_col(mout.at[chunk_id], mbuf.at[owner], msend.at[k], mrecv.at[owner],
                      (c + k) % ncol)

    sub = min(256, cb)

    def plan_of(b, qq, rb):
        parts = []
        for start in range(0, cb, sub):
            z = jnp.dot(qq, y_s[b, :, start:start + sub], preferred_element_type=F32)
            for t in range(0, sub, 128):
                val = z[:, t:t + 128] + jnp.maximum(
                    cb_s[b, 0:1, start + t:start + t + 128], rb)
                parts.append(jnp.exp2(val).astype(BF16))
        return jnp.concatenate(parts, axis=1)

    @pl.loop(0, ncol)
    def _(s):
        q = (c + ncol - 1 - s) % ncol
        base = pl.multiple_of(q * xs, xs)

        @pl.loop(0, half)
        def _(j):
            first = (r + nrow - 2 * j) % nrow
            second = (r + nrow - 2 * j - 1) % nrow

            @pl.when(s == 0)
            def _():
                for k, b in ((2 * j, first), (2 * j + 1, second)):
                    @pl.when(k > 0)
                    def _():
                        cp_copy(k, b).wait_recv()

                    put_cols(b, ct_s[b] + (1.0 / (EPS * LN2)) * cpbuf[b]
                             + log2(cbuf[b, 1:2]) - nu_col)

            qq = q_s[pl.ds(base, xs)]
            rb = rb_s[pl.ds(base, xs)]
            plan_a = plan_of(first, qq, rb)
            plan_b = plan_of(second, qq, rb)
            g_s[pl.ds(base, xs)] += (
                jnp.dot(plan_a, ft_s[first], preferred_element_type=F32)
                + jnp.dot(plan_b, ft_s[second], preferred_element_type=F32))

        gout[q] = g_s[pl.ds(base, xs), 0:128]
        mout[q] = g_s[pl.ds(base, xs), 128:256].T[0:8]

        @pl.when(s < ncol - 1)
        def _():
            g_copy(ncol - 1 - s, q, c).start()
            m_copy(ncol - 1 - s, q, c).start()

    for b in range(nrow):
        colpot_ref[b] = cpbuf[b]

    gbuf[c] = gout[c]
    mbuf[c] = mout[c]

    @pl.loop(1, ncol)
    def _(k):
        owner = (c + ncol - k) % ncol
        g_copy(k, c, owner).wait_recv()
        m_copy(k, c, owner).wait_recv()

    moments = sum(gbuf[k] for k in range(ncol))
    mass_row = sum(mbuf[k] for k in range(ncol))[0:1]
    mass = jnp.broadcast_to(mass_row, (128, xs)).T
    x, h = doubled(xbuf[c], lax.broadcasted_iota(jnp.int32, (xs, 128), 1))
    second = pltpu.roll(moments, 64, 1)
    grad = moments - x * mass
    curv = (second - 2.0 * x * moments + x * x * mass) / EPS + RIDGE
    damping = jnp.concatenate([damping_ref[...], damping_ref[...]], axis=1)
    new = h - damping * grad / curv
    mult_ref[...] = new.T[0:width]

    @pl.loop(1, ncol)
    def _(k):
        x_copy(k, c).wait_send()
        r_copy(k, c).wait_send()
        rm_copy(k, c).wait_send()
        g_copy(k, (c + k) % ncol, c).wait_send()
        m_copy(k, (c + k) % ncol, c).wait_send()

    @pl.loop(1, nrow)
    def _(k):
        cm_copy(k, (r + k) % nrow, r).wait_send()
        cp_copy(k, r).wait_send()

    @pl.loop(0, half)
    def _(k):
        for copy in w_copies(k, same(k)):
            copy.wait_send()

    @pl.loop(1, half)
    def _(k):
        for copy in z_copies(k, r):
            copy.wait_send()


def on_device(nrow, ncol, x_points, y_points, row_mass, col_mass, multipliers, col_potential,
              basket, damping):
    xs, width = x_points.shape
    cb = y_points.shape[0]
    rows = xs * ncol
    rmass = row_mass.astype(F32)[None, :]
    cmass = col_mass.astype(F32)[None, :]
    pot = col_potential.astype(F32)[None, :]
    half = nrow // 2
    dma = pltpu.SemaphoreType.DMA
    vmem = pltpu.VMEM
    whole = pl.BlockSpec(memory_space=pltpu.VMEM)
    row_pot, col_pot, mult = pl.pallas_call(
        functools.partial(kernel, nrow, ncol),
        out_shape=(jax.ShapeDtypeStruct((1, rows), F32),
                   jax.ShapeDtypeStruct((nrow, 1, cb), F32),
                   jax.ShapeDtypeStruct((width, xs), F32)),
        in_specs=[whole] * 8,
        out_specs=(whole,) * 3,
        scratch_shapes=[
            vmem((ncol, xs, 128), BF16), vmem((ncol, 1, xs), F32),
            vmem((nrow, width, cb), BF16), vmem((nrow, 2, cb), F32),
            vmem((ncol, 4, rows), F32), vmem((nrow, 4, cb), F32), vmem((nrow, 4, cb), F32),
            vmem((nrow, 1, cb), F32),
            vmem((ncol, xs, 128), F32), vmem((ncol, xs, 128), F32),
            vmem((ncol, 8, xs), F32), vmem((ncol, 8, xs), F32),
            vmem((rows, 256), BF16), vmem((rows, 128), F32), vmem((rows, 128), F32),
            vmem((rows, 128), F32), vmem((nrow, 256, cb), BF16), vmem((nrow, cb, 256), BF16),
            vmem((nrow, 8, cb), F32), vmem((nrow, 1, cb), F32),
            vmem((rows, 128), F32), vmem((rows, 128), F32), vmem((rows, cb), F32),
            vmem((rows, cb), F32), vmem((128, 128), F32), vmem((rows, 256), F32), vmem((rows, 128), F32),
            dma((ncol,)), dma((ncol,)), dma((ncol,)), dma((ncol,)),
            dma((half,)), dma((half,)), dma((nrow,)),
            dma((half,)), dma((half,)), dma((nrow,)),
            dma((ncol,)), dma((ncol,)), dma((nrow,)), dma((nrow,)),
            dma((nrow,)), dma((nrow,)), dma((ncol,)), dma((ncol,)),
            dma((ncol,)), dma((ncol,)),
        ],
        compiler_params=pltpu.CompilerParams(
            collective_id=0, has_side_effects=True, vmem_limit_bytes=56 * 1024 * 1024),
    )(x_points.T, multipliers.T, rmass, y_points.T, pot, cmass, basket[None, :], damping[None, :])
    return row_pot.reshape(rows), col_pot.reshape(nrow * cb), mult.T


def solution(mesh):
    placed = (
        P(("row", "col"), None),
        P(("col", "row"), None),
        P(("row", "col")),
        P(("col", "row")),
        P(("row", "col"), None),
        P(("col", "row")),
        P(),
        P(),
    )
    return jax.shard_map(
        functools.partial(on_device, mesh.shape["row"], mesh.shape["col"]),
        mesh=mesh,
        in_specs=placed,
        out_specs=(P("row"), P("col"), P(("row", "col"), None)),
        check_vma=False,
    )
```

```python
import functools
import math
import jax
import jax.numpy as jnp
from jax import lax
from jax.experimental import pallas as pl
from jax.experimental.pallas import tpu as pltpu
from jax.sharding import PartitionSpec as P

EPS = 0.5
KAPPA = 0.5
RIDGE = 1.0
L2E = math.log2(math.e)
LN2 = math.log(2.0)
SCALE = L2E / EPS
LOW = -1e30
F32 = jnp.float32
BF16 = jnp.bfloat16


def split3(value):
    one = value.astype(BF16).astype(F32)
    rest = value - one
    two = rest.astype(BF16).astype(F32)
    return one, two, rest - two


def log2(value):
    return jnp.log(value) * L2E


def kernel(
    nrow, ncol,
    xt_ref, mt_ref, rmass_ref, yt_ref, pot_ref, cmass_ref, basket_ref, damping_ref,
    rowpot_ref, colpot_ref, mult_ref,
    xbuf, rbuf, ybuf, cbuf, rowmsg, colout, colmsg, cpbuf, gout, gbuf, mout, mbuf,
    q_s, q3_s, rt_s, rb_s, y_s, ft_s, cb_s, ct_s, top_s, sum_s, za_s, zb_s, bc_s, g_s, f_s,
    xsend, xrecv, rsend, rrecv, zsend, wsend, yrecv, czsend, cwsend, crecv,
    rmsend, rmrecv, cmsend, cmrecv, cpsend, cprecv, gsend, grecv, msend, mrecv,
):
    r = lax.axis_index("row")
    c = lax.axis_index("col")
    xs = xt_ref.shape[1]
    cb = yt_ref.shape[1]
    width = yt_ref.shape[0]
    rows = xs * ncol
    half = nrow // 2
    pair = r % 2
    group = r // 2
    twin = r + 1 - 2 * pair

    def to_col(src, dst, send, recv, other):
        return pltpu.make_async_remote_copy(
            src_ref=src, dst_ref=dst, send_sem=send, recv_sem=recv,
            device_id=(r, other), device_id_type=pl.DeviceIdType.MESH)

    def to_row(src, dst, send, recv, other):
        return pltpu.make_async_remote_copy(
            src_ref=src, dst_ref=dst, send_sem=send, recv_sem=recv,
            device_id=(other, c), device_id_type=pl.DeviceIdType.MESH)

    barrier = pltpu.get_barrier_semaphore()

    @pl.loop(1, ncol)
    def _(k):
        pl.semaphore_signal(barrier, inc=1, device_id=(r, (c + k) % ncol),
                            device_id_type=pl.DeviceIdType.MESH)

    @pl.loop(1, nrow)
    def _(k):
        pl.semaphore_signal(barrier, inc=1, device_id=((r + k) % nrow, c),
                            device_id_type=pl.DeviceIdType.MESH)

    xbuf[c] = jnp.concatenate([xt_ref[...], mt_ref[...]], axis=0).astype(F32).T.astype(BF16)
    rbuf[c] = rmass_ref[...]
    ybuf[r] = yt_ref[...]
    cbuf[r, 0:1] = SCALE * pot_ref[...] + log2(cmass_ref[...])
    cbuf[r, 1:2] = cmass_ref[...]
    basket_row = jnp.concatenate([basket_ref[...], jnp.zeros((1, 128 - width), F32)], axis=1)
    pl.semaphore_wait(barrier, nrow + ncol - 2)

    def x_copy(k, owner):
        return to_col(xbuf.at[owner], xbuf.at[owner], xsend.at[k], xrecv.at[owner],
                      (c + k) % ncol)

    def r_copy(k, owner):
        return to_col(rbuf.at[owner], rbuf.at[owner], rsend.at[k], rrecv.at[owner],
                      (c + k) % ncol)

    @pl.loop(1, ncol)
    def _(k):
        x_copy(k, c).start()
        r_copy(k, c).start()

    def same(k):
        return ((group + 2 * half - k) % half) * 2 + pair

    def other(k):
        return ((group + half - k) % half) * 2 + 1 - pair

    def z_copies(k, block):
        goal = ((group + k) % half) * 2 + pair
        return (to_row(cbuf.at[block], cbuf.at[block], czsend.at[k], crecv.at[block], goal),
                to_row(ybuf.at[block], ybuf.at[block], zsend.at[k], yrecv.at[block], goal))

    def w_copies(k, block):
        return (to_row(cbuf.at[block], cbuf.at[block], cwsend.at[k], crecv.at[block], twin),
                to_row(ybuf.at[block], ybuf.at[block], wsend.at[k], yrecv.at[block], twin))

    for copy in w_copies(0, r):
        copy.start()

    @pl.loop(1, half)
    def _(k):
        for copy in z_copies(k, r):
            copy.start()

    bc_s[...] = jnp.broadcast_to(basket_row, (128, 128)).T
    one_row = lax.broadcasted_iota(jnp.int32, (128, cb), 0) == 0
    ones = jnp.where(one_row, 1.0, 0.0).astype(BF16)

    @pl.loop(0, nrow)
    def _(b):
        y_s[b, 3 * width:4 * width] = jnp.zeros((width, cb), BF16)
        ft_s[b, 128:256] = ones

    top_s[...] = jnp.full(top_s.shape, LOW, F32)
    sum_s[...] = jnp.zeros(sum_s.shape, F32)

    def prepare_block(b):
        y16 = ybuf[b]
        yf = y16.astype(F32)
        sq = yf * yf
        y_s[b, 0:width] = y16
        y_s[b, width:2 * width] = y16
        y_s[b, 2 * width:3 * width] = y16
        ft_s[b, 0:width] = y16
        ft_s[b, width:2 * width] = sq.astype(BF16)
        ct_s[b] = -(SCALE * KAPPA / width) * jnp.sum(sq, axis=0, keepdims=True)
        wide = jnp.concatenate([bc_s[0:width]] * (cb // 128), axis=1)
        basket = SCALE * jnp.sum(yf * wide, axis=0, keepdims=True)
        cb_s[b] = jnp.broadcast_to(basket, (8, cb))

    def doubled(both, lane):
        both = both.astype(F32)
        swapped = pltpu.roll(both, 64, 1)
        return jnp.where(lane < 64, both, swapped), jnp.where(lane < 64, swapped, both)

    def put_cols(b, value):
        row = lax.broadcasted_iota(jnp.int32, (16, cb), 0)
        one, two, three = split3(value)
        ext = jnp.where(row < 3, 1.0, 0.0)
        ext = jnp.where(row == 3, one, ext)
        ext = jnp.where(row == 4, two, ext)
        ext = jnp.where(row == 5, three, ext)
        y_s[b, 3 * width:3 * width + 16] = ext.astype(BF16)

    def put_rows(start, size, value):
        lane = lax.broadcasted_iota(jnp.int32, (size, 128), 1)
        one, two, three = split3(value)
        ext = jnp.where((lane >= 67) & (lane < 70), 1.0, q3_s[pl.ds(start, size)])
        ext = jnp.where(lane == 64, one, ext)
        ext = jnp.where(lane == 65, two, ext)
        ext = jnp.where(lane == 66, three, ext)
        q_s[pl.ds(start, size), 128:256] = ext.astype(BF16)

    prepare_block(r)

    @pl.loop(1, ncol)
    def _(k):
        owner = (c + ncol - k) % ncol
        x_copy(k, owner).wait_recv()
        r_copy(k, owner).wait_recv()

    @pl.loop(0, ncol)
    def _(k):
        lane = lax.broadcasted_iota(jnp.int32, (xs, 128), 1)
        x, h = doubled(xbuf[k], lane)
        one, two, three = split3(SCALE * (h + (2.0 * KAPPA / width) * x))
        here = pl.ds(k * xs, xs)
        xb = x * basket_row
        q_s[here, 0:128] = jnp.where(lane < 64, one, two).astype(BF16)
        q3_s[here] = jnp.where(lane < 64, three, 0.0)
        term = -0.5 * (h * x + (KAPPA / width) * (x * x)) - xb
        rt = jnp.broadcast_to(SCALE * jnp.sum(term, axis=1, keepdims=True), (xs, 128))
        rb_s[here] = jnp.broadcast_to(SCALE * jnp.sum(xb, axis=1, keepdims=True), (xs, 128))
        rt_s[here] = rt
        put_rows(k * xs, xs, rt)

    chunk = min(256, cb)
    tiles = cb // 128

    row_chunk = min(256, rows)

    def row_block(b):
        put_cols(b, ct_s[b] + cbuf[b, 0:1])
        size = 32

        def dots(start):
            here = slice(start, start + row_chunk)
            za_s[here] = jnp.dot(q_s[here], y_s[b], preferred_element_type=F32)

        dots(0)
        for start in range(0, rows, row_chunk):
            if start + row_chunk < rows:
                dots(start + row_chunk)

            def step(i, _, start=start):
                here = pl.ds(pl.multiple_of(start + i * size, size), size)
                rb = rb_s[here]
                vals = []
                for t in range(tiles):
                    span = slice(t * 128, (t + 1) * 128)
                    vals.append(za_s[here, span] + jnp.maximum(cb_s[b, 0:1, span], rb))
                old = top_s[here]
                top = functools.reduce(jnp.maximum, vals, old)
                total = sum_s[here] * jnp.exp2(old - top)
                for val in vals:
                    total = total + jnp.exp2(val - top)
                top_s[here] = top
                sum_s[here] = total
                return 0

            lax.fori_loop(0, row_chunk // size, step, 0, unroll=True)

    @pl.loop(0, half)
    def _(k):
        first = same(k)

        @pl.when(k > 0)
        def _():
            for copy in z_copies(k, first):
                copy.wait_recv()
            for copy in w_copies(k, first):
                copy.start()
            prepare_block(first)

        row_block(first)
        second = other(k)
        for copy in w_copies(k, second):
            copy.wait_recv()
        prepare_block(second)
        row_block(second)

    tops = top_s[...].T
    sums = sum_s[...].T
    top = jnp.max(tops, axis=0, keepdims=True)
    total = jnp.sum(sums * jnp.exp2(tops - top), axis=0, keepdims=True)
    nu_part = cbuf[0, 1:2]
    for b in range(1, nrow):
        nu_part = nu_part + cbuf[b, 1:2]
    nu_part = jnp.sum(nu_part, axis=1, keepdims=True)
    rowmsg[c, 0:1] = top
    rowmsg[c, 1:2] = total
    rowmsg[c, 2:3] = jnp.broadcast_to(nu_part, (1, rows))
    rowmsg[c, 3:4] = jnp.zeros((1, rows), F32)

    def rm_copy(k, owner):
        return to_col(rowmsg.at[owner], rowmsg.at[owner], rmsend.at[k], rmrecv.at[owner],
                      (c + k) % ncol)

    @pl.loop(1, ncol)
    def _(k):
        rm_copy(k, c).start()

    masses = jnp.concatenate([rbuf[k] for k in range(ncol)], axis=1)
    mu_part = jnp.broadcast_to(jnp.sum(masses, axis=1, keepdims=True), (1, cb))
    top_s[...] = rt_s[...] + jnp.broadcast_to(log2(masses), (128, rows)).T

    @pl.loop(1, ncol)
    def _(k):
        rm_copy(k, (c + ncol - k) % ncol).wait_recv()

    top = functools.reduce(jnp.maximum, [rowmsg[k, 0:1] for k in range(ncol)])
    total = sum(rowmsg[k, 1:2] * jnp.exp2(rowmsg[k, 0:1] - top) for k in range(ncol))
    nu_log = log2(sum(rowmsg[k, 2:3] for k in range(ncol)))
    f_row = nu_log - (top + log2(total))
    rowpot_ref[...] = (EPS * LN2) * f_row
    nu_col = jnp.broadcast_to(nu_log[:, 0:1], (1, cb))
    f_col = jnp.broadcast_to(f_row, (128, rows)).T
    f_s[...] = rt_s[...] + f_col
    put_rows(0, rows, top_s[...] + f_col)

    def cm_copy(k, block, owner):
        return to_row(colout.at[block], colmsg.at[owner], cmsend.at[k], cmrecv.at[owner],
                      (r + k) % nrow)

    size = 64

    def col_rows(k):
        b = (r + 1 + k) % nrow
        put_cols(b, ct_s[b])
        return b

    def col_dots(b, z_s, start):
        cols = slice(start, start + chunk)
        z_s[:, cols] = jnp.dot(q_s[...], y_s[b, :, cols], preferred_element_type=F32)

    def col_part(b, z_s, start):
        span = slice(start, start + chunk)
        lo = cb_s[b, :, span]

        def step(i, carry):
            old, total = carry
            vals = []
            for t in range(size // 8):
                here = pl.ds(pl.multiple_of(i * size + t * 8, 8), 8)
                wide = jnp.concatenate([rb_s[here]] * (chunk // 128), axis=1)
                vals.append(z_s[here, span] + jnp.maximum(lo, wide))
            top = functools.reduce(jnp.maximum, vals, old)
            total = total * jnp.exp2(old - top)
            for val in vals:
                total = total + jnp.exp2(val - top)
            return top, total

        tops, sums = lax.fori_loop(
            0, rows // size, step,
            (jnp.full((8, chunk), LOW, F32), jnp.zeros((8, chunk), F32)), unroll=True)
        top = jnp.max(tops, axis=0, keepdims=True)
        colout[b, 0:1, span] = top
        colout[b, 1:2, span] = jnp.sum(sums * jnp.exp2(tops - top), axis=0, keepdims=True)

    def col_turn(k, now, ahead):
        b = (r + 1 + k) % nrow
        later = col_rows(k + 1)
        for start in range(0, cb, chunk):
            col_dots(later, ahead, start)
            col_part(b, now, start)
        colout[b, 2:3] = mu_part
        colout[b, 3:4] = jnp.zeros((1, cb), F32)

        @pl.when(k < nrow - 1)
        def _():
            cm_copy(k + 1, b, r).start()

    start_block = col_rows(0)
    for start in range(0, cb, chunk):
        col_dots(start_block, za_s, start)

    @pl.loop(0, half)
    def _(j):
        col_turn(2 * j, za_s, zb_s)
        col_turn(2 * j + 1, zb_s, za_s)

    colmsg[r] = colout[r]
    put_rows(0, rows, f_s[...])

    @pl.loop(1, nrow)
    def _(k):
        cm_copy(k, r, (r + nrow - k) % nrow).wait_recv()

    top = functools.reduce(jnp.maximum, [colmsg[k, 0:1] for k in range(nrow)])
    total = sum(colmsg[k, 1:2] * jnp.exp2(colmsg[k, 0:1] - top) for k in range(nrow))
    mu_log = log2(sum(colmsg[k, 2:3] for k in range(nrow)))
    cpbuf[r] = (EPS * LN2) * (mu_log - (top + log2(total)))

    def cp_copy(k, owner):
        return to_row(cpbuf.at[owner], cpbuf.at[owner], cpsend.at[k], cprecv.at[owner],
                      (r + k) % nrow)

    @pl.loop(1, nrow)
    def _(k):
        cp_copy(k, r).start()

    g_s[...] = jnp.zeros(g_s.shape, F32)

    def g_copy(k, chunk_id, owner):
        return to_col(gout.at[chunk_id], gbuf.at[owner], gsend.at[k], grecv.at[owner],
                      (c + k) % ncol)

    def m_copy(k, chunk_id, owner):
        return to_col(mout.at[chunk_id], mbuf.at[owner], msend.at[k], mrecv.at[owner],
                      (c + k) % ncol)

    sub = min(256, cb)

    def moments_of(plan, b):
        return lax.dot_general(plan, ft_s[b], (((1,), (1,)), ((), ())),
                               preferred_element_type=F32)

    def plan_of(b, qq, rb):
        parts = []
        for start in range(0, cb, sub):
            z = jnp.dot(qq, y_s[b, :, start:start + sub], preferred_element_type=F32)
            for t in range(0, sub, 128):
                val = z[:, t:t + 128] + jnp.maximum(
                    cb_s[b, 0:1, start + t:start + t + 128], rb)
                parts.append(jnp.exp2(val).astype(BF16))
        return jnp.concatenate(parts, axis=1)

    @pl.loop(0, ncol)
    def _(s):
        q = (c + ncol - 1 - s) % ncol
        base = pl.multiple_of(q * xs, xs)

        @pl.loop(0, half)
        def _(j):
            first = (r + nrow - 2 * j) % nrow
            second = (r + nrow - 2 * j - 1) % nrow

            @pl.when(s == 0)
            def _():
                for k, b in ((2 * j, first), (2 * j + 1, second)):
                    @pl.when(k > 0)
                    def _():
                        cp_copy(k, b).wait_recv()

                    put_cols(b, ct_s[b] + (1.0 / (EPS * LN2)) * cpbuf[b]
                             + log2(cbuf[b, 1:2]) - nu_col)

            qq = q_s[pl.ds(base, xs)]
            rb = rb_s[pl.ds(base, xs)]
            plan_a = plan_of(first, qq, rb)
            plan_b = plan_of(second, qq, rb)
            g_s[pl.ds(base, xs)] += (
                moments_of(plan_a, first) + moments_of(plan_b, second))

        gout[q] = g_s[pl.ds(base, xs), 0:128]
        mout[q] = g_s[pl.ds(base, xs), 128:256].T[0:8]

        @pl.when(s < ncol - 1)
        def _():
            g_copy(ncol - 1 - s, q, c).start()
            m_copy(ncol - 1 - s, q, c).start()

    for b in range(nrow):
        colpot_ref[b] = cpbuf[b]

    gbuf[c] = gout[c]
    mbuf[c] = mout[c]

    @pl.loop(1, ncol)
    def _(k):
        owner = (c + ncol - k) % ncol
        g_copy(k, c, owner).wait_recv()
        m_copy(k, c, owner).wait_recv()

    moments = sum(gbuf[k] for k in range(ncol))
    mass_row = sum(mbuf[k] for k in range(ncol))[0:1]
    mass = jnp.broadcast_to(mass_row, (128, xs)).T
    x, h = doubled(xbuf[c], lax.broadcasted_iota(jnp.int32, (xs, 128), 1))
    second = pltpu.roll(moments, 64, 1)
    grad = moments - x * mass
    curv = (second - 2.0 * x * moments + x * x * mass) / EPS + RIDGE
    damping = jnp.concatenate([damping_ref[...], damping_ref[...]], axis=1)
    new = h - damping * grad / curv
    mult_ref[...] = new.T[0:width]

    @pl.loop(1, ncol)
    def _(k):
        x_copy(k, c).wait_send()
        r_copy(k, c).wait_send()
        rm_copy(k, c).wait_send()
        g_copy(k, (c + k) % ncol, c).wait_send()
        m_copy(k, (c + k) % ncol, c).wait_send()

    @pl.loop(1, nrow)
    def _(k):
        cm_copy(k, (r + k) % nrow, r).wait_send()
        cp_copy(k, r).wait_send()

    @pl.loop(0, half)
    def _(k):
        for copy in w_copies(k, same(k)):
            copy.wait_send()

    @pl.loop(1, half)
    def _(k):
        for copy in z_copies(k, r):
            copy.wait_send()


def on_device(nrow, ncol, x_points, y_points, row_mass, col_mass, multipliers, col_potential,
              basket, damping):
    xs, width = x_points.shape
    cb = y_points.shape[0]
    rows = xs * ncol
    rmass = row_mass.astype(F32)[None, :]
    cmass = col_mass.astype(F32)[None, :]
    pot = col_potential.astype(F32)[None, :]
    half = nrow // 2
    dma = pltpu.SemaphoreType.DMA
    vmem = pltpu.VMEM
    whole = pl.BlockSpec(memory_space=pltpu.VMEM)
    row_pot, col_pot, mult = pl.pallas_call(
        functools.partial(kernel, nrow, ncol),
        out_shape=(jax.ShapeDtypeStruct((1, rows), F32),
                   jax.ShapeDtypeStruct((nrow, 1, cb), F32),
                   jax.ShapeDtypeStruct((width, xs), F32)),
        in_specs=[whole] * 8,
        out_specs=(whole,) * 3,
        scratch_shapes=[
            vmem((ncol, xs, 128), BF16), vmem((ncol, 1, xs), F32),
            vmem((nrow, width, cb), BF16), vmem((nrow, 2, cb), F32),
            vmem((ncol, 4, rows), F32), vmem((nrow, 4, cb), F32), vmem((nrow, 4, cb), F32),
            vmem((nrow, 1, cb), F32),
            vmem((ncol, xs, 128), F32), vmem((ncol, xs, 128), F32),
            vmem((ncol, 8, xs), F32), vmem((ncol, 8, xs), F32),
            vmem((rows, 256), BF16), vmem((rows, 128), F32), vmem((rows, 128), F32),
            vmem((rows, 128), F32), vmem((nrow, 256, cb), BF16), vmem((nrow, 256, cb), BF16),
            vmem((nrow, 8, cb), F32), vmem((nrow, 1, cb), F32),
            vmem((rows, 128), F32), vmem((rows, 128), F32), vmem((rows, cb), F32),
            vmem((rows, cb), F32), vmem((128, 128), F32), vmem((rows, 256), F32), vmem((rows, 128), F32),
            dma((ncol,)), dma((ncol,)), dma((ncol,)), dma((ncol,)),
            dma((half,)), dma((half,)), dma((nrow,)),
            dma((half,)), dma((half,)), dma((nrow,)),
            dma((ncol,)), dma((ncol,)), dma((nrow,)), dma((nrow,)),
            dma((nrow,)), dma((nrow,)), dma((ncol,)), dma((ncol,)),
            dma((ncol,)), dma((ncol,)),
        ],
        compiler_params=pltpu.CompilerParams(
            collective_id=0, has_side_effects=True, vmem_limit_bytes=56 * 1024 * 1024),
    )(x_points.T, multipliers.T, rmass, y_points.T, pot, cmass, basket[None, :], damping[None, :])
    return row_pot.reshape(rows), col_pot.reshape(nrow * cb), mult.T


def solution(mesh):
    placed = (
        P(("row", "col"), None),
        P(("col", "row"), None),
        P(("row", "col")),
        P(("col", "row")),
        P(("row", "col"), None),
        P(("col", "row")),
        P(),
        P(),
    )
    return jax.shard_map(
        functools.partial(on_device, mesh.shape["row"], mesh.shape["col"]),
        mesh=mesh,
        in_specs=placed,
        out_specs=(P("row"), P("col"), P(("row", "col"), None)),
        check_vma=False,
    )
```
